32 devices in a mesh: grp: 2 (over y), dp: 8 (over z, x), ep: 2 (over core).
Axes of the slice: x: 2, y: 2, z: 4, core: 2. Of those that a mesh axis runs over, the one named last changes fastest.
Arguments:
- cache: bfloat16 [64, 24, 36864], P(('grp', 'dp', 'ep')), parts along dimension 0, may hold values from -4.5 to 4.5
- queries: bfloat16 [64, 1, 73728], P(('grp', 'dp', 'ep')), parts along dimension 0, may hold values from -14 to 14
- kv_new: bfloat16 [64, 1, 576], P(('grp', 'dp', 'ep')), parts along dimension 0, may hold values from -4.5 to 4.5
- lengths: int32 [64], P('grp'), parts along dimension 0, may hold values from 1 to 1535, as said below
- move_slot: int32 [32], P('grp'), parts along dimension 0, may hold values from 0 to 2, as said below
- hidden: bfloat16 [64, 1, 7168], P(('grp', 'dp', 'ep')), parts along dimension 0, may hold values from -6 to 6
- expert_ids: int32 [64, 1, 8], P('grp'), parts along dimension 0, may hold values from 0 to 15, all different within a row
- router: bfloat16 [16, 7168], replicated, may hold values from -0.0625 to 0.0625
- routed_gate: bfloat16 [16384, 7168], P(('dp', 'ep')), may hold values from -0.0625 to 0.0625
- routed_up: bfloat16 [16384, 7168], P(('dp', 'ep')), may hold values from -0.0625 to 0.0625
- routed_down: bfloat16 [16384, 7168], P(('dp', 'ep')), may hold values from -0.1875 to 0.1875
- shared_gate: bfloat16 [2048, 7168], P(('dp', 'ep')), may hold values from -0.0625 to 0.0625
- shared_up: bfloat16 [2048, 7168], P(('dp', 'ep')), may hold values from -0.0625 to 0.0625
- shared_down: bfloat16 [2048, 7168], P(('dp', 'ep')), may hold values from -0.125 to 0.125
Outputs:
- attn_out: bfloat16 [64, 1, 65536], P(('grp', 'dp', 'ep')), parts along dimension 0
- moe_out: bfloat16 [64, 1, 7168], P(('grp', 'dp', 'ep')), parts along dimension 0
The draws below stay inside these ranges and needn't reach their ends.
There are 2 independent parts, one for each index of `grp`. The reference program is written for one: setup_inputs(seed, part) draws one part's arguments, and reference() takes and returns one part's arrays. A program takes and returns all parts, laid end to end along the dimension named above; an argument that names none is the same for every part. Nothing has to cross between parts.
Inputs may be any that keep to these rules, and one draw needn't show every extreme that they name: `lengths`: positions of a slot's cache at or above its length hold no data. `move_slot`: 2 means that no request of the group moves; a group and its partner are both 2 or both below it.
All inputs are finite; a program needn't handle non-finite values.
Results may differ from the reference program's by a relative error of at most 0.009.
Values may be sent and summed in bfloat16 or wider, within the bound.
A program may use at most 128 MiB of HBM per device.

```python
import jax
import jax.numpy as jnp
from jax import lax

H = 128
DL = 512
DK = 576
D = 7168
FF = 1024
FF_SH = 2048
EXPERTS = 16
TOPK = 8
PAGE = 64
R_DEV = 2
STEPS = 1
PR = 24
REQUESTS = 32
TOK = 32
N_DP = 8
N_EP = 2


def request_plan(key):
    top_length = PR * PAGE - STEPS
    short_lengths = jax.random.randint(jax.random.fold_in(key, 201), (REQUESTS,), 1, top_length // 4 + 1)
    long_lengths = jax.random.randint(jax.random.fold_in(key, 202), (REQUESTS,), top_length // 2, top_length + 1)
    heavy_pick = jax.random.randint(jax.random.fold_in(key, 203), (REQUESTS,), 0, 4) == 0
    lengths = jnp.where(heavy_pick, long_lengths, short_lengths)
    peak_slot = jax.random.randint(jax.random.fold_in(key, 204), (), 0, REQUESTS)
    lengths = jnp.where(jnp.arange(REQUESTS) == peak_slot, top_length, lengths).astype(jnp.int32)
    group_count = REQUESTS // R_DEV
    group_ids = jnp.arange(group_count, dtype=jnp.int32)
    partners = (group_ids // N_EP + N_DP // 2) % N_DP * N_EP + group_ids % N_EP
    grouped = lengths.reshape(group_count, R_DEV)
    loads = jnp.sum(grouped, axis=1)
    longest = jnp.max(grouped, axis=1)
    shortest = jnp.min(grouped, axis=1)
    other_loads = loads[partners]
    heavier = loads > other_loads
    lighter = loads < other_loads
    gains = jnp.where(heavier, longest - shortest[partners], longest[partners] - shortest)
    moving = (heavier | lighter) & (gains > 0) & (gains < jnp.abs(loads - other_loads))
    chosen_slots = jnp.where(heavier, jnp.argmax(grouped, axis=1), jnp.argmin(grouped, axis=1))
    move_slot = jnp.where(moving, chosen_slots, R_DEV).astype(jnp.int32)
    return (lengths, move_slot)


def draw_lengths(key, part):
    lengths, move_slot = request_plan(key)
    return lengths


def draw_move_slot(key, part):
    lengths, move_slot = request_plan(key)
    return move_slot


def draw_kv_new(key, part):
    own_key = jax.random.fold_in(key, 3)
    values = jnp.clip(jax.random.normal(own_key, (REQUESTS, STEPS, DK), jnp.float32), -4.5, 4.5)
    return values.astype(jnp.bfloat16)


def draw_queries(key, part):
    own_key = jax.random.fold_in(key, 4)
    values = jnp.clip(0.6 * jax.random.normal(own_key, (REQUESTS, STEPS, H, DK), jnp.float32), -3.6, 3.6)
    return values.reshape(REQUESTS, STEPS, H * DK).astype(jnp.bfloat16)


def shard_levels(key, extent, cuts, least, top_value):
    def one(dim, shards_of):
        steps = jax.random.uniform(jax.random.fold_in(jax.random.fold_in(key, 6), dim), (shards_of,), jnp.float32, least / len(cuts), top_value / len(cuts))
        return jnp.repeat(jnp.exp(steps), extent[dim] // shards_of).reshape((-1,) + (1,) * (len(extent) - dim - 1))

    factor_of = one(*cuts[0])
    for cut in cuts[1:]:
        factor_of = factor_of * one(*cut)
    return factor_of


def different_ones(key, rows, number_of, top, lift):
    order = jax.random.permutation(jax.random.fold_in(key, 1), number_of)
    pull = order
    for power in range(3):
        pull = pull * pull // number_of
    pull = pull * lift // number_of
    lots = jax.random.randint(jax.random.fold_in(key, 2), (rows, number_of), 0, 4096) + pull
    sure = jax.random.permutation(jax.random.fold_in(key, 3), rows)[jnp.arange(number_of) % rows]
    lots = jnp.where(jnp.arange(rows)[:, None] == sure[None, :], 1 << 14, lots)
    priority = lots * number_of + jnp.arange(number_of)
    return lax.top_k(priority.astype(jnp.int32), top)[1].astype(jnp.int32)


def normal_values(rng, shape, scale, reach, pieces=(), kind=jnp.bfloat16):
    drawn = jax.random.normal(rng, shape, jnp.float32) * scale
    if len(pieces) > 0:
        drawn = shard_levels(rng, shape, pieces, -0.22, 0.18) * drawn
    return jnp.clip(drawn, min=-reach, max=reach).astype(kind)


def setup_inputs(seed: int = 0, part: int = 0) -> dict:
    key_list = jax.random.split(jax.random.key(seed), 15)
    part_keys = jax.random.split(jax.random.fold_in(key_list[14], part), 15)
    return {
        "cache": normal_values(part_keys[0], (REQUESTS, PR, PAGE * DK), 1.0, 4.5, ((0, 16),)),
        "queries": draw_queries(jax.random.fold_in(jax.random.fold_in(key_list[14], part), 71), part),
        "kv_new": draw_kv_new(jax.random.fold_in(jax.random.fold_in(key_list[14], part), 71), part),
        "lengths": draw_lengths(jax.random.fold_in(jax.random.fold_in(key_list[14], part), 71), part),
        "move_slot": draw_move_slot(jax.random.fold_in(jax.random.fold_in(key_list[14], part), 71), part),
        "hidden": normal_values(part_keys[5], (REQUESTS, STEPS, D), 1.0, 6.0, ((0, 16),)),
        "expert_ids": different_ones(part_keys[6], REQUESTS * STEPS, EXPERTS, TOPK, 4096).reshape((REQUESTS, STEPS, TOPK)),
        "router": normal_values(key_list[7], (EXPERTS, D), D ** -0.5, 0.0625),
        "routed_gate": normal_values(key_list[8], (EXPERTS * FF, D), D ** -0.5, 0.0625, ((0, 16),)),
        "routed_up": normal_values(key_list[9], (EXPERTS * FF, D), D ** -0.5, 0.0625, ((0, 16),)),
        "routed_down": normal_values(key_list[10], (EXPERTS * FF, D), FF ** -0.5, 0.1875, ((0, 16),)),
        "shared_gate": normal_values(key_list[11], (FF_SH, D), D ** -0.5, 0.0625, ((0, 16),)),
        "shared_up": normal_values(key_list[12], (FF_SH, D), D ** -0.5, 0.0625, ((0, 16),)),
        "shared_down": normal_values(key_list[13], (FF_SH, D), FF_SH ** -0.5, 0.125, ((0, 16),)),
    }


SCORE_SCALE = 192.0 ** -0.5
ROUTE_SCALE = 2.5


def source_slots(move_slot):
    group_ids = jnp.arange(N_DP * N_EP, dtype=jnp.int32)
    partners = ((group_ids // N_EP + N_DP // 2) % N_DP) * N_EP + group_ids % N_EP
    slot_ids = jnp.arange(REQUESTS, dtype=jnp.int32)
    owners = slot_ids // R_DEV
    within = slot_ids % R_DEV
    others = partners[owners]
    swapped = move_slot[owners] == within
    return jnp.where(swapped, others * R_DEV + move_slot[others], slot_ids).astype(jnp.int32)


def attend_request(cache_rows, query_rows, fresh_rows, length):
    capacity = PR * PAGE
    key_rows = jnp.concatenate([cache_rows, fresh_rows], axis=0)
    scores = jnp.einsum("thk,pk->thp", query_rows, key_rows) * SCORE_SCALE
    position = jnp.arange(capacity + STEPS, dtype=jnp.int32)
    step_ids = jnp.arange(STEPS, dtype=jnp.int32)
    visible = (position[None, :] < length) | ((position[None, :] >= capacity) & (position[None, :] - capacity <= step_ids[:, None]))
    scores = jnp.where(visible[:, None, :], scores, -jnp.inf)
    probs = jax.nn.softmax(scores, axis=-1).astype(jnp.bfloat16)
    values = key_rows[:, :DL]
    output = jnp.einsum("thp,pk->thk", probs.astype(jnp.float32), values)
    return output.astype(jnp.bfloat16)


def reference(cache, queries, kv_new, lengths, move_slot, hidden, expert_ids, router, routed_gate, routed_up, routed_down, shared_gate, shared_up, shared_down):
    sources = source_slots(move_slot)

    def serve(slot_id):
        root = sources[slot_id].astype(jnp.int32)
        cache_rows = lax.dynamic_index_in_dim(cache, root, 0, keepdims=False).reshape(PR * PAGE, DK).astype(jnp.float32)
        query_rows = lax.dynamic_index_in_dim(queries, slot_id, 0, keepdims=False).reshape(STEPS, H, DK).astype(jnp.float32)
        fresh_rows = lax.dynamic_index_in_dim(kv_new, slot_id, 0, keepdims=False).astype(jnp.float32)
        length = lax.dynamic_index_in_dim(lengths, root, 0, keepdims=False)
        return attend_request(cache_rows, query_rows, fresh_rows, length).reshape(STEPS, H * DL)

    attn_out = lax.map(serve, jnp.arange(REQUESTS, dtype=jnp.int32))

    tokens = hidden.reshape(TOK, D)
    chosen_ids = expert_ids.reshape(TOK, TOPK)
    logits = jnp.dot(tokens, router.T, preferred_element_type=jnp.float32)
    sigmas = jax.nn.sigmoid(logits)
    expert_table = jnp.arange(EXPERTS, dtype=jnp.int32)
    chosen = jnp.sum((chosen_ids[:, :, None] == expert_table[None, None, :]).astype(jnp.float32), axis=1)
    picked = sigmas * chosen
    weights = ROUTE_SCALE * picked / jnp.sum(picked, axis=1, keepdims=True)

    def add_expert(total, stacked):
        gate_rows, up_rows, down_rows, expert_weight = stacked
        gate_value = jnp.dot(tokens, gate_rows.T, preferred_element_type=jnp.float32)
        up_value = jnp.dot(tokens, up_rows.T, preferred_element_type=jnp.float32)
        activation = (expert_weight[:, None] * jax.nn.silu(gate_value) * up_value).astype(jnp.bfloat16)
        return total + jnp.dot(activation, down_rows, preferred_element_type=jnp.float32), None

    stacked = (routed_gate.reshape(EXPERTS, FF, D), routed_up.reshape(EXPERTS, FF, D), routed_down.reshape(EXPERTS, FF, D), weights.T)
    total, unused = lax.scan(add_expert, jnp.zeros((TOK, D), jnp.float32), stacked)
    shared_gate_value = jnp.dot(tokens, shared_gate.T, preferred_element_type=jnp.float32)
    shared_up_value = jnp.dot(tokens, shared_up.T, preferred_element_type=jnp.float32)
    shared_act = (jax.nn.silu(shared_gate_value) * shared_up_value).astype(jnp.bfloat16)
    total = total + jnp.dot(shared_act, shared_down, preferred_element_type=jnp.float32)
    moe_out = total.astype(jnp.bfloat16).reshape(REQUESTS, STEPS, D)
    return attn_out, moe_out
```

```python
import functools

import jax
import jax.numpy as jnp
from jax import lax
from jax.experimental import pallas as pl
from jax.experimental.pallas import tpu as pltpu
from jax.sharding import PartitionSpec as P

DL = 512
FF = 1024
SCORE_SCALE = 192.0 ** (-0.5)
ROUTE_SCALE = 2.5
NEGATIVE = -1e30
CH = 8
WIDTHS = (384, 256, 256)
MESH = pl.DeviceIdType.MESH
F32 = jnp.float32
BF16 = jnp.bfloat16


def contract_last(a, b):
    return lax.dot_general(a, b, (((1,), (1,)), ((), ())), preferred_element_type=F32)


def kernel(
    n_dp, rchunk,
    scal, qk_ref, hid_ref, ids_ref, pos_ref,
    cache_h, router_h, rg_h, ru_h, rd_h, sg_h, su_h, sd_h,
    attn_ref, moe_ref,
    cache_s, router_s, g_s, u_s, d_s,
    xg, xf, x_s, act_s, kk, qsend, qrecv, osend, orecv,
    ybuf, yown, r1, zs, fs, zb0, zb1, zb2, q20, q21, q22,
    w_sem, sx, sf, rx, sq, rq, so, ro, s1, rr1, s2, r2sem,
):
    j0 = lax.axis_index("dp")
    e0 = lax.axis_index("ep")
    sib = 1 - e0
    partner = lax.rem(j0 + n_dp // 2, n_dp)
    rows = rg_h.shape[0]
    srows = sg_h.shape[0]
    d_model = rg_h.shape[1]
    ntok = x_s.shape[0]
    half = ntok // 2
    zbs, r2s = (zb0, zb1, zb2), (q20, q21, q22)

    copies = []

    def fetch(src, dst):
        c = pltpu.make_async_copy(src, dst, w_sem.at[len(copies)])
        c.start()
        copies.append(c)
        return c

    c_cache = fetch(cache_h, cache_s)
    c_router = fetch(router_h, router_s)
    gu = []
    for r in range(0, rows, rchunk):
        gu.append((
            r, rchunk, True,
            fetch(rg_h.at[pl.ds(r, rchunk), :], g_s.at[pl.ds(r, rchunk), :]),
            fetch(ru_h.at[pl.ds(r, rchunk), :], u_s.at[pl.ds(r, rchunk), :]),
        ))
    gu.append((
        rows, srows, False,
        fetch(sg_h, g_s.at[pl.ds(rows, srows), :]),
        fetch(su_h, u_s.at[pl.ds(rows, srows), :]),
    ))
    downs = []
    base = 0
    for w in WIDTHS:
        cols = pl.ds(base, CH * w)
        downs.append((
            base, w,
            fetch(rd_h.at[:, cols], d_s.at[pl.ds(0, rows), cols]),
            fetch(sd_h.at[:, cols], d_s.at[pl.ds(rows, srows), cols]),
        ))
        base += CH * w

    barrier = pltpu.get_barrier_semaphore()

    def greet(k, _):
        pl.semaphore_signal(barrier, inc=1, device_id={"dp": lax.rem(j0 + k, n_dp)}, device_id_type=MESH)
        return 0

    lax.fori_loop(1, n_dp, greet, 0)
    pl.semaphore_signal(barrier, inc=1, device_id={"ep": sib}, device_id_type=MESH)
    pl.semaphore_wait(barrier, n_dp)

    def x_copy(k):
        return pltpu.make_async_remote_copy(
            src_ref=hid_ref, dst_ref=xg.at[e0, j0], send_sem=sx.at[k], recv_sem=rx.at[e0, j0],
            device_id={"dp": lax.rem(j0 + k, n_dp)}, device_id_type=MESH)

    x_sib = pltpu.make_async_remote_copy(
        src_ref=hid_ref, dst_ref=xg.at[e0, j0], send_sem=sx.at[0], recv_sem=rx.at[e0, j0],
        device_id={"ep": sib}, device_id_type=MESH)

    def x_send(k, _):
        x_copy(k).start()
        return 0

    lax.fori_loop(1, n_dp, x_send, 0)
    x_sib.start()
    xg[e0, j0] = hid_ref[...]

    own_move = scal[0]
    moving = own_move < 2
    slot_b = jnp.where(own_move == 0, 0, 1)
    slot_a = 1 - slot_b
    nq = qsend.shape[0] - 16
    pairs = kk.shape[0] // cache_s.shape[1]
    pages = cache_s.shape[1]
    wide = kk.shape[1]
    win = (wide // 2 + 127) // 128 * 128
    off = wide - win
    shift = wide // 2 - off
    dk = wide // 2

    def attend(qk, slot, length):
        def retile(t, _):
            parts = [
                cache_s[slot, :, pl.ds(pl.multiple_of((2 * t + i) * wide, 128), wide)].astype(F32)
                for i in range(2)
            ]
            kk[pl.ds(pl.multiple_of(2 * pages * t, 16), 2 * pages), :] = (
                jnp.concatenate(parts, axis=0).astype(BF16))
            return 0

        lax.fori_loop(0, pairs // 2, retile, 0)
        qf = qk.astype(F32)
        lane = lax.broadcasted_iota(jnp.int32, (nq, win), 1)
        q_even = jnp.where(lane < dk, qf[:nq, :win], 0.0)
        q_odd = jnp.where(lane >= shift, qf[:nq, off:], 0.0)
        qe = jnp.concatenate([q_even, pltpu.roll(q_odd, win - shift, 1)], axis=0)
        qo = jnp.concatenate([pltpu.roll(q_even, shift, 1), q_odd], axis=0)
        kv = qf[nq:nq + 1, :win]
        s_n = jnp.sum(qe * kv, axis=1, keepdims=True) * SCORE_SCALE
        pos = pos_ref[0:1, :]
        s_e = jnp.where(pos < length, contract_last(qe.astype(BF16), kk[:, :win]) * SCORE_SCALE, NEGATIVE)
        s_o = jnp.where(pos + 1 < length, contract_last(qo.astype(BF16), kk[:, off:]) * SCORE_SCALE, NEGATIVE)
        top = jnp.maximum(jnp.max(s_e, axis=1, keepdims=True), jnp.max(s_o, axis=1, keepdims=True))
        top = jnp.maximum(top, s_n)
        p_e, p_o, p_n = jnp.exp(s_e - top), jnp.exp(s_o - top), jnp.exp(s_n - top)
        total = jnp.sum(p_e, axis=1, keepdims=True) + jnp.sum(p_o, axis=1, keepdims=True) + p_n
        o_e = jnp.dot(p_e.astype(BF16), kk[:, :DL], preferred_element_type=F32)
        o_o = jnp.dot(p_o.astype(BF16), kk[:, off:], preferred_element_type=F32)
        out = o_e + pltpu.roll(o_o, win - shift, 1)[:, :DL] + p_n * kv[:, :DL]
        out = out / total
        return jnp.concatenate([out[:nq], out[nq:]], axis=1).astype(BF16)

    qsend[...] = qk_ref[slot_b]
    c_cache.wait()
    out_a = attend(qk_ref[slot_a], slot_a, scal[1 + slot_a])
    attn_ref[0] = out_a

    def arrived(e, j):
        return pltpu.make_async_remote_copy(
            src_ref=hid_ref, dst_ref=xg.at[e, j], send_sem=sx.at[0], recv_sem=rx.at[e, j],
            device_id={"ep": sib}, device_id_type=MESH)

    def fwd_copy(k):
        j = lax.rem(j0 + n_dp - k, n_dp)
        return pltpu.make_async_remote_copy(
            src_ref=xg.at[e0, j], dst_ref=xg.at[e0, j], send_sem=sf.at[k], recv_sem=rx.at[e0, j],
            device_id={"ep": sib}, device_id_type=MESH)

    def pass_on(k, _):
        arrived(e0, lax.rem(j0 + n_dp - k, n_dp)).wait_recv()
        fwd_copy(k).start()
        return 0

    lax.fori_loop(1, n_dp, pass_on, 0)

    q_copy = pltpu.make_async_remote_copy(
        src_ref=qsend, dst_ref=qrecv, send_sem=sq, recv_sem=rq,
        device_id={"dp": partner}, device_id_type=MESH)
    q_copy.start()

    def settle(k, _):
        arrived(sib, lax.rem(j0 + n_dp - k, n_dp)).wait_recv()
        return 0

    lax.fori_loop(0, n_dp, settle, 0)

    tiles = xf.shape[0]
    gathered = xg[...].reshape(xf.shape[1], tiles * 128).astype(F32)
    for i in range(tiles):
        xf[i] = gathered[:, i * 128:(i + 1) * 128]
    for c in range(CH):
        for i in range(tiles):
            at = (c * tiles + i) * 128
            x_s[:, at:at + 128] = xf[i, pl.ds(c, ntok, stride=CH), :].astype(BF16)

    c_router.wait()
    n_exp = router_s.shape[0]
    sig = 1.0 / (1.0 + jnp.exp(-contract_last(x_s[...], router_s[...])))
    table = lax.broadcasted_iota(jnp.int32, (ntok, n_exp), 1)
    ids = ids_ref[...]
    chosen = jnp.zeros((ntok, n_exp), F32)
    for k in range(ids.shape[1]):
        chosen += jnp.where(ids[:, k:k + 1] == table, 1.0, 0.0)
    picked = sig * chosen
    expert = (j0 * 2 + e0) * rows // FF
    mine = jnp.sum(jnp.where(table == expert, picked, 0.0), axis=1, keepdims=True)
    row_weight = ROUTE_SCALE * mine / jnp.sum(picked, axis=1, keepdims=True)

    for r, n, routed, cg, cu in gu:
        cg.wait()
        g = contract_last(x_s[...], g_s[pl.ds(r, n), :])
        cu.wait()
        u = contract_last(x_s[...], u_s[pl.ds(r, n), :])
        act = g / (1.0 + jnp.exp(-g)) * u
        if routed:
            act = row_weight * act
        act_s[:, r:r + n] = act.astype(BF16)

    q_copy.wait_recv()
    q_b = jnp.where(moving, qrecv[...].astype(F32), qsend[...].astype(F32)).astype(BF16)
    out_b = attend(q_b, slot_b, scal[1 + slot_b])
    osend[...] = out_b
    o_copy = pltpu.make_async_remote_copy(
        src_ref=osend, dst_ref=orecv, send_sem=so, recv_sem=ro,
        device_id={"dp": partner}, device_id_type=MESH)
    o_copy.start()

    def first_copy(p):
        b, w = downs[p][0], downs[p][1]
        cols = pl.ds(b, CH * w)
        return pltpu.make_async_remote_copy(
            src_ref=ybuf.at[pl.ds(pl.multiple_of(sib * half, 16), half), cols],
            dst_ref=r1.at[:, cols], send_sem=s1.at[p], recv_sem=rr1.at[p],
            device_id={"ep": sib}, device_id_type=MESH)

    def second_copy(p, k):
        j = lax.rem(j0 + k, n_dp)
        return pltpu.make_async_remote_copy(
            src_ref=zbs[p].at[j], dst_ref=r2s[p].at[j0], send_sem=s2.at[p, k], recv_sem=r2sem.at[p, j0],
            device_id={"dp": j}, device_id_type=MESH)

    def second_arrived(p, j):
        return pltpu.make_async_remote_copy(
            src_ref=zbs[p].at[j], dst_ref=r2s[p].at[j], send_sem=s2.at[p, 0], recv_sem=r2sem.at[p, j],
            device_id={"dp": j}, device_id_type=MESH)

    def combine(p):
        b, w = downs[p][0], downs[p][1]
        first_copy(p).wait_recv()
        z = yown[:, b:b + CH * w] + r1[:, b:b + CH * w].astype(F32)
        for c in range(CH):
            for i in range(w // 128):
                at = c * w + i * 128
                zs[i, pl.ds(c, half, stride=CH), :] = z[:, at:at + 128]
        for i in range(w // 128):
            zbs[p][:, :, i * 128:(i + 1) * 128] = zs[i].astype(BF16).reshape(n_dp, -1, 128)

        def send(k, _):
            second_copy(p, k).start()
            return 0

        lax.fori_loop(1, n_dp, send, 0)

    def finish(p):
        b, w = downs[p][0], downs[p][1]

        def add(k, total):
            j = lax.rem(j0 + k, n_dp)
            second_arrived(p, j).wait_recv()
            return total + r2s[p][j].astype(F32)

        total = lax.fori_loop(1, n_dp, add, zbs[p][j0].astype(F32))
        for i in range(w // 128):
            fs[i] = total[:, i * 128:(i + 1) * 128]
        for c in range(CH):
            for i in range(w // 128):
                at = b + c * w + i * 128
                moe_ref[:, at:at + 128] = fs[i, pl.ds(c, fs.shape[1] // CH, stride=CH), :]

    act_all = act_s[...]
    for p, (b, w, c1, c2) in enumerate(downs):
        c1.wait()
        c2.wait()
        y = jnp.dot(act_all, d_s[:, b:b + CH * w], preferred_element_type=F32)
        ybuf[:, b:b + CH * w] = y.astype(BF16)
        yown[:, b:b + CH * w] = jnp.where(e0 == 0, y[:half], y[half:])
        first_copy(p).start()
        if p > 0:
            combine(p - 1)
    combine(len(downs) - 1)
    for p in range(len(downs)):
        finish(p)

    o_copy.wait_recv()
    res_a = attn_ref[0].astype(F32)
    res_b = jnp.where(moving, orecv[...].astype(F32), osend[...].astype(F32))
    attn_ref[0] = jnp.where(slot_a == 0, res_a, res_b).astype(BF16)
    attn_ref[1] = jnp.where(slot_a == 0, res_b, res_a).astype(BF16)

    x_sib.wait_send()
    q_copy.wait_send()
    o_copy.wait_send()

    def drain(k, _):
        x_copy(k).wait_send()
        fwd_copy(k).wait_send()
        for p in range(len(downs)):
            second_copy(p, k).wait_send()
        return 0

    lax.fori_loop(1, n_dp, drain, 0)
    for p in range(len(downs)):
        first_copy(p).wait_send()


def local(cache, queries, kv_new, lengths, move_slot, hidden, expert_ids, router,
          routed_gate, routed_up, routed_down, shared_gate, shared_up, shared_down):
    n_dp = lax.axis_size("dp")
    n_ep = lax.axis_size("ep")
    slots, pages, page_len = cache.shape
    dk = kv_new.shape[-1]
    d_model = hidden.shape[-1]
    own_tok = hidden.shape[0] * hidden.shape[1]
    ntok = own_tok * n_dp * n_ep
    half = ntok // 2
    rows, srows = routed_gate.shape[0], shared_gate.shape[0]
    all_rows = rows + srows
    wide = 2 * dk
    nq = queries.shape[-1] // wide
    pairs = page_len // wide
    device = lax.axis_index(("dp", "ep"))
    own_lengths = lax.dynamic_slice_in_dim(lengths, device * slots, slots, 0)
    own_move = lax.dynamic_slice_in_dim(move_slot, device, 1, 0)
    scal = jnp.concatenate([own_move, own_lengths])
    kv = jnp.pad(kv_new.reshape(slots, 1, dk), ((0, 0), (0, 15), (0, wide - dk)))
    qk = jnp.concatenate([queries.reshape(slots, nq, wide), kv], axis=1)
    hid = hidden.reshape(own_tok * CH, d_model // CH)
    ids = expert_ids.reshape(n_dp, n_ep, own_tok, -1).transpose(1, 0, 2, 3).reshape(ntok, -1)
    index = jnp.arange(pairs * pages, dtype=jnp.int32)
    pos = jnp.broadcast_to((index % pages * (2 * pairs) + index // pages * 2)[None], (8, pairs * pages))
    wmax = max(WIDTHS)
    np_ = len(WIDTHS)
    rchunk = min(rows, 256)
    ncopy = 2 + 2 * (rows // rchunk + 1) + 2 * np_
    vm = pl.BlockSpec(memory_space=pltpu.VMEM)
    hb = pl.BlockSpec(memory_space=pl.ANY)
    dma = pltpu.SemaphoreType.DMA
    attn, moe = pl.pallas_call(
        functools.partial(kernel, n_dp, rchunk),
        out_shape=(
            jax.ShapeDtypeStruct((slots, nq, 2 * DL), BF16),
            jax.ShapeDtypeStruct((own_tok, d_model), F32),
        ),
        in_specs=[pl.BlockSpec(memory_space=pltpu.SMEM), vm, vm, vm, vm] + [hb] * 8,
        out_specs=(vm, vm),
        scratch_shapes=[
            pltpu.VMEM(cache.shape, BF16),
            pltpu.VMEM(router.shape, BF16),
            pltpu.VMEM((all_rows, d_model), BF16),
            pltpu.VMEM((all_rows, d_model), BF16),
            pltpu.VMEM((all_rows, d_model), BF16),
            pltpu.VMEM((n_ep, n_dp, own_tok * CH, d_model // CH), BF16),
            pltpu.VMEM((d_model // CH // 128, ntok * CH, 128), F32),
            pltpu.VMEM((ntok, d_model), BF16),
            pltpu.VMEM((ntok, all_rows), BF16),
            pltpu.VMEM((pairs * pages, wide), BF16),
            pltpu.VMEM((nq + 16, wide), BF16),
            pltpu.VMEM((nq + 16, wide), BF16),
            pltpu.VMEM((nq, 2 * DL), BF16),
            pltpu.VMEM((nq, 2 * DL), BF16),
            pltpu.VMEM((ntok, d_model), BF16),
            pltpu.VMEM((half, d_model), F32),
            pltpu.VMEM((half, d_model), BF16),
            pltpu.VMEM((wmax // 128, half * CH, 128), F32),
            pltpu.VMEM((wmax // 128, own_tok * CH, 128), F32),
        ]
        + [pltpu.VMEM((n_dp, own_tok * CH, w), BF16) for w in WIDTHS] * 2
        + [
            dma((ncopy,)), dma((n_dp,)), dma((n_dp,)), dma((n_ep, n_dp)),
            dma, dma, dma, dma,
            dma((np_,)), dma((np_,)), dma((np_, n_dp)), dma((np_, n_dp)),
        ],
        compiler_params=pltpu.CompilerParams(
            collective_id=0, has_side_effects=True, vmem_limit_bytes=63 * 1024 * 1024),
    )(scal, qk, hid, ids, pos, cache, router, routed_gate, routed_up, routed_down,
      shared_gate, shared_up, shared_down)
    return (attn.reshape(slots, 1, nq * 2 * DL), moe.astype(BF16).reshape(hidden.shape))


def solution(mesh):
    row = P(("grp", "dp", "ep"), None, None)
    weight = P(("dp", "ep"), None)
    in_specs = (row, row, row, P("grp"), P("grp"), row, P("grp", None, None), P()) + (weight,) * 6
    return jax.shard_map(local, mesh=mesh, in_specs=in_specs, out_specs=(row, row), check_vma=False)
```

```python
import functools

import jax
import jax.numpy as jnp
from jax import lax
from jax.experimental import pallas as pl
from jax.experimental.pallas import tpu as pltpu
from jax.sharding import PartitionSpec as P

DL = 512
FF = 1024
SCORE_SCALE = 192.0 ** (-0.5)
ROUTE_SCALE = 2.5
NEGATIVE = -1e30
CH = 8
WIDTHS = (384, 256, 256)
MESH = pl.DeviceIdType.MESH
F32 = jnp.float32
BF16 = jnp.bfloat16


def contract_last(a, b):
    return lax.dot_general(a, b, (((1,), (1,)), ((), ())), preferred_element_type=F32)


def kernel(
    n_dp, rchunk,
    len_ref, move_ref, q_ref, kv_ref, hid_ref, ids_ref,
    cache_h, router_h, rg_h, ru_h, rd_h, sg_h, su_h, sd_h,
    attn_ref, moe_ref,
    cache_s, router_s, g_s, u_s, d_s,
    hf, hsend, xg, xf, x_s, act_s, kk, qsend, qrecv, kvsend, kvrecv, osend, orecv,
    ybuf, yown, r1, zs, fs, zb0, zb1, zb2, q20, q21, q22,
    w_sem, sx, sf, sg, rx, sq, rq, skv, rkv, so, ro, s1, rr1, s2, r2sem,
):
    j0 = lax.axis_index("dp")
    e0 = lax.axis_index("ep")
    sib = 1 - e0
    partner = lax.rem(j0 + n_dp // 2, n_dp)
    rows = rg_h.shape[0]
    srows = sg_h.shape[0]
    d_model = rg_h.shape[1]
    ntok = x_s.shape[0]
    half = ntok // 2
    zbs, r2s = (zb0, zb1, zb2), (q20, q21, q22)

    copies = []

    def fetch(src, dst):
        c = pltpu.make_async_copy(src, dst, w_sem.at[len(copies)])
        c.start()
        copies.append(c)
        return c

    c_cache = fetch(cache_h, cache_s)
    c_router = fetch(router_h, router_s)
    gu = []
    for r in range(0, rows, rchunk):
        gu.append((
            r, rchunk, True,
            fetch(rg_h.at[pl.ds(r, rchunk), :], g_s.at[pl.ds(r, rchunk), :]),
            fetch(ru_h.at[pl.ds(r, rchunk), :], u_s.at[pl.ds(r, rchunk), :]),
        ))
    gu.append((
        rows, srows, False,
        fetch(sg_h, g_s.at[pl.ds(rows, srows), :]),
        fetch(su_h, u_s.at[pl.ds(rows, srows), :]),
    ))
    downs = []
    base = 0
    for w in WIDTHS:
        cols = pl.ds(base, CH * w)
        downs.append((
            base, w,
            fetch(rd_h.at[:, cols], d_s.at[pl.ds(0, rows), cols]),
            fetch(sd_h.at[:, cols], d_s.at[pl.ds(rows, srows), cols]),
        ))
        base += CH * w

    tiles = hf.shape[0]
    own = hid_ref[...].astype(F32)
    own_tok = own.shape[0]
    for c in range(CH):
        for i in range(tiles):
            at = (c * tiles + i) * 128
            hf[i, pl.ds(c, own_tok, stride=CH), :] = own[:, at:at + 128]
    for i in range(tiles):
        hsend[:, i * 128:(i + 1) * 128] = hf[i].astype(BF16)

    barrier = pltpu.get_barrier_semaphore()

    def greet(k, _):
        pl.semaphore_signal(barrier, inc=1, device_id={"dp": lax.rem(j0 + k, n_dp)}, device_id_type=MESH)
        return 0

    lax.fori_loop(1, n_dp, greet, 0)
    pl.semaphore_signal(barrier, inc=1, device_id={"ep": sib}, device_id_type=MESH)
    pl.semaphore_wait(barrier, n_dp)

    n_out = n_dp // 2
    out0 = j0 // 2
    in0 = lax.rem(j0, 2)
    across = out0 * 2 + 1 - in0

    def peer(k):
        return lax.rem(out0 + k, n_out) * 2 + in0

    def x_copy(src, j, sem, target):
        return pltpu.make_async_remote_copy(
            src_ref=src, dst_ref=xg.at[e0, j], send_sem=sem, recv_sem=rx.at[e0, j],
            device_id=target, device_id_type=MESH)

    def x_out(k):
        return x_copy(hsend, j0, sx.at[k], {"dp": peer(k)})

    def x_over(k):
        src = hsend if k is None else xg.at[e0, peer(k)]
        j = j0 if k is None else peer(k)
        return x_copy(src, j, sf.at[0 if k is None else k], {"dp": across})

    def x_sib(j, src):
        return x_copy(src, j, sg.at[j], {"ep": sib})

    def arrived(e, j):
        return pltpu.make_async_remote_copy(
            src_ref=hsend, dst_ref=xg.at[e, j], send_sem=sx.at[0], recv_sem=rx.at[e, j],
            device_id={"ep": sib}, device_id_type=MESH)

    def send_out(k, _):
        x_out(k).start()
        return 0

    lax.fori_loop(1, n_out, send_out, 0)
    x_over(None).start()
    x_sib(j0, hsend).start()
    xg[e0, j0] = hsend[...]

    device = j0 * 2 + e0
    own_move = move_ref[device]
    moving = own_move < 2
    slot_b = jnp.where(own_move == 0, 0, 1)
    slot_a = 1 - slot_b
    nq = qsend.shape[0]
    pairs = kk.shape[0] // cache_s.shape[1]
    pages = cache_s.shape[1]
    wide = kk.shape[1]
    win = (wide // 2 + 127) // 128 * 128
    off = wide - win
    shift = wide // 2 - off
    dk = wide // 2

    def attend(q, kv, slot):
        length = len_ref[device * 2 + slot]

        def retile(t, _):
            parts = [
                cache_s[slot, :, pl.ds(pl.multiple_of((2 * t + i) * wide, 128), wide)].astype(F32)
                for i in range(2)
            ]
            kk[pl.ds(pl.multiple_of(2 * pages * t, 16), 2 * pages), :] = (
                jnp.concatenate(parts, axis=0).astype(BF16))
            return 0

        lax.fori_loop(0, pairs // 2, retile, 0)
        qf = q.astype(F32)
        lane = lax.broadcasted_iota(jnp.int32, (nq, win), 1)
        q_even = jnp.where(lane < dk, qf[:nq, :win], 0.0)
        q_odd = jnp.where(lane >= shift, qf[:nq, off:], 0.0)
        qe = jnp.concatenate([q_even, pltpu.roll(q_odd, win - shift, 1)], axis=0)
        qo = jnp.concatenate([pltpu.roll(q_even, shift, 1), q_odd], axis=0)
        s_n = jnp.sum(qe * kv, axis=1, keepdims=True) * SCORE_SCALE
        index = lax.broadcasted_iota(jnp.int32, (1, kk.shape[0]), 1)
        pair = ((index.astype(F32) + 0.5) * (1.0 / pages)).astype(jnp.int32)
        pos = (index - pair * pages) * (2 * pairs) + pair * 2
        s_e = jnp.where(pos < length, contract_last(qe.astype(BF16), kk[:, :win]) * SCORE_SCALE, NEGATIVE)
        s_o = jnp.where(pos + 1 < length, contract_last(qo.astype(BF16), kk[:, off:]) * SCORE_SCALE, NEGATIVE)
        top = jnp.maximum(jnp.max(s_e, axis=1, keepdims=True), jnp.max(s_o, axis=1, keepdims=True))
        top = jnp.maximum(top, s_n)
        p_e, p_o, p_n = jnp.exp(s_e - top), jnp.exp(s_o - top), jnp.exp(s_n - top)
        total = jnp.sum(p_e, axis=1, keepdims=True) + jnp.sum(p_o, axis=1, keepdims=True) + p_n
        o_e = jnp.dot(p_e.astype(BF16), kk[:, :DL], preferred_element_type=F32)
        o_o = jnp.dot(p_o.astype(BF16), kk[:, off:], preferred_element_type=F32)
        out = o_e + pltpu.roll(o_o, win - shift, 1)[:, :DL] + p_n * kv[:, :DL]
        out = out / total
        return jnp.concatenate([out[:nq], out[nq:]], axis=1).astype(BF16)

    qsend[...] = q_ref[slot_b]
    kvs = jnp.concatenate([kv_ref[...].astype(F32), jnp.zeros((kv_ref.shape[0], win - dk), F32)], axis=1)
    kv_b = jnp.where(slot_b == 0, kvs[0:1], kvs[1:2])
    kv_a = jnp.where(slot_b == 0, kvs[1:2], kvs[0:1])
    kvsend[...] = jnp.broadcast_to(kv_b, kvsend.shape).astype(BF16)
    q_copy = pltpu.make_async_remote_copy(
        src_ref=qsend, dst_ref=qrecv, send_sem=sq, recv_sem=rq,
        device_id={"dp": partner}, device_id_type=MESH)
    kv_copy = pltpu.make_async_remote_copy(
        src_ref=kvsend, dst_ref=kvrecv, send_sem=skv, recv_sem=rkv,
        device_id={"dp": partner}, device_id_type=MESH)

    def pass_out(k, _):
        arrived(e0, peer(n_out - k)).wait_recv()
        x_over(n_out - k).start()
        x_sib(peer(n_out - k), xg.at[e0, peer(n_out - k)]).start()
        return 0

    lax.fori_loop(1, n_out, pass_out, 0)
    kv_copy.start()
    q_copy.start()

    def pass_in(k, _):
        j = lax.rem(out0 + n_out - k, n_out) * 2 + 1 - in0
        arrived(e0, j).wait_recv()
        x_sib(j, xg.at[e0, j]).start()
        return 0

    lax.fori_loop(0, n_out, pass_in, 0)

    def settle(k, _):
        arrived(sib, lax.rem(j0 + n_dp - k, n_dp)).wait_recv()
        return 0

    lax.fori_loop(0, n_dp, settle, 0)

    gathered = xg[...].reshape(xf.shape[1], tiles * 128).astype(F32)
    for i in range(tiles):
        xf[i] = gathered[:, i * 128:(i + 1) * 128]
    for c in range(CH):
        for i in range(tiles):
            at = (c * tiles + i) * 128
            x_s[:, at:at + 128] = xf[i, pl.ds(c, ntok, stride=CH), :].astype(BF16)

    c_router.wait()
    n_exp = router_s.shape[0]
    sig = 1.0 / (1.0 + jnp.exp(-contract_last(x_s[...], router_s[...])))
    table = lax.broadcasted_iota(jnp.int32, (ntok, n_exp), 1)
    ids = ids_ref[...]
    table_t = lax.broadcasted_iota(jnp.int32, (n_exp, ntok), 0)
    chosen_t = jnp.zeros((n_exp, ntok), F32)
    for k in range(ids.shape[0]):
        chosen_t += jnp.where(ids[k:k + 1, :] == table_t, 1.0, 0.0)
    row = lax.broadcasted_iota(jnp.int32, (ntok, ntok), 0)
    core = jnp.where(row >= half, 1, 0)
    rest = row - core * half
    token = rest + (rest & ~(own_tok - 1)) + core * own_tok
    perm = jnp.where(token == lax.broadcasted_iota(jnp.int32, (ntok, ntok), 1), 1.0, 0.0)
    chosen = contract_last(perm.astype(BF16), chosen_t.astype(BF16))
    picked = sig * chosen
    expert = (j0 * 2 + e0) * rows // FF
    mine = jnp.sum(jnp.where(table == expert, picked, 0.0), axis=1, keepdims=True)
    row_weight = ROUTE_SCALE * mine / jnp.sum(picked, axis=1, keepdims=True)

    def hidden_units(r, n, routed, cg, cu):
        cg.wait()
        g = contract_last(x_s[...], g_s[pl.ds(r, n), :])
        cu.wait()
        u = contract_last(x_s[...], u_s[pl.ds(r, n), :])
        act = g / (1.0 + jnp.exp(-g)) * u
        if routed:
            act = row_weight * act
        act_s[:, r:r + n] = act.astype(BF16)

    early = min(2, len(gu))
    for args in gu[:early]:
        hidden_units(*args)

    c_cache.wait()
    kv_copy.wait_recv()
    q_copy.wait_recv()
    q_b = jnp.where(moving, qrecv[...].astype(F32), qsend[...].astype(F32))
    kv_b = jnp.where(moving, kvrecv[0:1, :].astype(F32), kv_b)
    osend[...] = attend(q_b, kv_b, slot_b)
    o_copy = pltpu.make_async_remote_copy(
        src_ref=osend, dst_ref=orecv, send_sem=so, recv_sem=ro,
        device_id={"dp": partner}, device_id_type=MESH)
    o_copy.start()

    for args in gu[early:]:
        hidden_units(*args)

    def first_copy(p):
        b, w = downs[p][0], downs[p][1]
        cols = pl.ds(b, CH * w)
        return pltpu.make_async_remote_copy(
            src_ref=ybuf.at[pl.ds(pl.multiple_of(sib * half, 16), half), cols],
            dst_ref=r1.at[:, cols], send_sem=s1.at[p], recv_sem=rr1.at[p],
            device_id={"ep": sib}, device_id_type=MESH)

    def second_copy(p, k):
        j = lax.rem(j0 + k, n_dp)
        return pltpu.make_async_remote_copy(
            src_ref=zbs[p].at[j], dst_ref=r2s[p].at[j0], send_sem=s2.at[p, k], recv_sem=r2sem.at[p, j0],
            device_id={"dp": j}, device_id_type=MESH)

    def second_arrived(p, j):
        return pltpu.make_async_remote_copy(
            src_ref=zbs[p].at[j], dst_ref=r2s[p].at[j], send_sem=s2.at[p, 0], recv_sem=r2sem.at[p, j],
            device_id={"dp": j}, device_id_type=MESH)

    def combine(p):
        b, w = downs[p][0], downs[p][1]
        first_copy(p).wait_recv()
        z = yown[:, b:b + CH * w] + r1[:, b:b + CH * w].astype(F32)
        for c in range(CH):
            for i in range(w // 128):
                at = c * w + i * 128
                zs[i, pl.ds(c, half, stride=CH), :] = z[:, at:at + 128]
        for i in range(w // 128):
            zbs[p][:, :, i * 128:(i + 1) * 128] = zs[i].astype(BF16).reshape(n_dp, -1, 128)

        def send(k, _):
            second_copy(p, k).start()
            return 0

        lax.fori_loop(1, n_dp, send, 0)

    def finish(p):
        b, w = downs[p][0], downs[p][1]

        def add(k, total):
            j = lax.rem(j0 + k, n_dp)
            second_arrived(p, j).wait_recv()
            return total + r2s[p][j].astype(F32)

        total = lax.fori_loop(1, n_dp, add, zbs[p][j0].astype(F32))
        for i in range(w // 128):
            fs[i] = total[:, i * 128:(i + 1) * 128]
        for c in range(CH):
            for i in range(w // 128):
                at = b + c * w + i * 128
                moe_ref[:, at:at + 128] = fs[i, pl.ds(c, own_tok, stride=CH), :].astype(BF16)

    act_all = act_s[...]
    for p, (b, w, c1, c2) in enumerate(downs):
        c1.wait()
        c2.wait()
        y = jnp.dot(act_all, d_s[:, b:b + CH * w], preferred_element_type=F32)
        ybuf[:, b:b + CH * w] = y.astype(BF16)
        yown[:, b:b + CH * w] = jnp.where(e0 == 0, y[:half], y[half:])
        first_copy(p).start()
        if p > 0:
            combine(p - 1)
    combine(len(downs) - 1)
    out_a = attend(q_ref[slot_a], kv_a, slot_a)
    for p in range(len(downs)):
        finish(p)

    o_copy.wait_recv()
    res_a = out_a.astype(F32)
    res_b = jnp.where(moving, orecv[...].astype(F32), osend[...].astype(F32))
    attn_ref[0] = jnp.where(slot_a == 0, res_a, res_b).astype(BF16)
    attn_ref[1] = jnp.where(slot_a == 0, res_b, res_a).astype(BF16)

    q_copy.wait_send()
    kv_copy.wait_send()
    o_copy.wait_send()
    x_over(None).wait_send()

    def drain_out(k, _):
        x_out(k).wait_send()
        x_over(k).wait_send()
        return 0

    lax.fori_loop(1, n_out, drain_out, 0)

    def drain_sib(j, _):
        x_sib(j, hsend).wait_send()
        return 0

    lax.fori_loop(0, n_dp, drain_sib, 0)

    def drain(k, _):
        for p in range(len(downs)):
            second_copy(p, k).wait_send()
        return 0

    lax.fori_loop(1, n_dp, drain, 0)
    for p in range(len(downs)):
        first_copy(p).wait_send()


def local(cache, queries, kv_new, lengths, move_slot, hidden, expert_ids, router,
          routed_gate, routed_up, routed_down, shared_gate, shared_up, shared_down):
    n_dp = lax.axis_size("dp")
    n_ep = lax.axis_size("ep")
    slots, pages, page_len = cache.shape
    dk = kv_new.shape[-1]
    d_model = hidden.shape[-1]
    own_tok = hidden.shape[0] * hidden.shape[1]
    ntok = own_tok * n_dp * n_ep
    half = ntok // 2
    rows, srows = routed_gate.shape[0], shared_gate.shape[0]
    all_rows = rows + srows
    wide = 2 * dk
    nq = queries.shape[-1] // wide
    pairs = page_len // wide
    win = (dk + 127) // 128 * 128
    wmax = max(WIDTHS)
    np_ = len(WIDTHS)
    rchunk = min(rows, 256)
    ncopy = 2 + 2 * (rows // rchunk + 1) + 2 * np_
    vm = pl.BlockSpec(memory_space=pltpu.VMEM)
    hb = pl.BlockSpec(memory_space=pl.ANY)
    dma = pltpu.SemaphoreType.DMA
    attn, moe = pl.pallas_call(
        functools.partial(kernel, n_dp, rchunk),
        out_shape=(
            jax.ShapeDtypeStruct((slots, nq, 2 * DL), BF16),
            jax.ShapeDtypeStruct((own_tok, d_model), BF16),
        ),
        in_specs=[pl.BlockSpec(memory_space=pltpu.SMEM)] * 2 + [vm] * 4 + [hb] * 8,
        out_specs=(vm, vm),
        scratch_shapes=[
            pltpu.VMEM(cache.shape, BF16),
            pltpu.VMEM(router.shape, BF16),
            pltpu.VMEM((all_rows, d_model), BF16),
            pltpu.VMEM((all_rows, d_model), BF16),
            pltpu.VMEM((all_rows, d_model), BF16),
            pltpu.VMEM((d_model // CH // 128, own_tok * CH, 128), F32),
            pltpu.VMEM((own_tok * CH, d_model // CH), BF16),
            pltpu.VMEM((n_ep, n_dp, own_tok * CH, d_model // CH), BF16),
            pltpu.VMEM((d_model // CH // 128, ntok * CH, 128), F32),
            pltpu.VMEM((ntok, d_model), BF16),
            pltpu.VMEM((ntok, all_rows), BF16),
            pltpu.VMEM((pairs * pages, wide), BF16),
            pltpu.VMEM((nq, wide), BF16),
            pltpu.VMEM((nq, wide), BF16),
            pltpu.VMEM((16, win), BF16),
            pltpu.VMEM((16, win), BF16),
            pltpu.VMEM((nq, 2 * DL), BF16),
            pltpu.VMEM((nq, 2 * DL), BF16),
            pltpu.VMEM((ntok, d_model), BF16),
            pltpu.VMEM((half, d_model), F32),
            pltpu.VMEM((half, d_model), BF16),
            pltpu.VMEM((wmax // 128, half * CH, 128), F32),
            pltpu.VMEM((wmax // 128, own_tok * CH, 128), F32),
        ]
        + [pltpu.VMEM((n_dp, own_tok * CH, w), BF16) for w in WIDTHS] * 2
        + [
            dma((ncopy,)), dma((n_dp,)), dma((n_dp,)), dma((n_dp,)), dma((n_ep, n_dp)),
            dma, dma, dma, dma, dma, dma,
            dma((np_,)), dma((np_,)), dma((np_, n_dp)), dma((np_, n_dp)),
        ],
        compiler_params=pltpu.CompilerParams(
            collective_id=0, has_side_effects=True, vmem_limit_bytes=63 * 1024 * 1024),
    )(lengths, move_slot, queries.reshape(slots, nq, wide), kv_new.reshape(slots, dk),
      hidden.reshape(own_tok, d_model), expert_ids.reshape(ntok, -1).T, cache, router, routed_gate, routed_up, routed_down,
      shared_gate, shared_up, shared_down)
    return (attn.reshape(slots, 1, nq * 2 * DL), moe.reshape(hidden.shape))


def solution(mesh):
    row = P(("grp", "dp", "ep"), None, None)
    weight = P(("dp", "ep"), None)
    in_specs = (row, row, row, P("grp"), P("grp"), row, P("grp", None, None), P()) + (weight,) * 6
    return jax.shard_map(local, mesh=mesh, in_specs=in_specs, out_specs=(row, row), check_vma=False)
```

```python
import functools

import jax
import jax.numpy as jnp
from jax import lax
from jax.experimental import pallas as pl
from jax.experimental.pallas import tpu as pltpu
from jax.sharding import PartitionSpec as P

DL = 512
FF = 1024
SCORE_SCALE = 192.0 ** (-0.5)
ROUTE_SCALE = 2.5
NEGATIVE = -1e30
CH = 8
WIDTHS = (384, 384, 128)
MESH = pl.DeviceIdType.MESH
F32 = jnp.float32
BF16 = jnp.bfloat16


def contract_last(a, b):
    return lax.dot_general(a, b, (((1,), (1,)), ((), ())), preferred_element_type=F32)


def kernel(
    n_dp, rchunk,
    len_ref, move_ref, q_ref, kv_ref, hid_ref, ids_ref,
    cache_h, router_h, rg_h, ru_h, rd_h, sg_h, su_h, sd_h,
    attn_ref, moe_ref,
    cache_s, router_s, g_s, u_s, d_s,
    hf, hsend, xg, xf, x_s, act_s, kk, qsend, qrecv, kvsend, kvrecv, osend, orecv,
    ybuf, yown, r1, zs, fs, zb0, zb1, zb2, q20, q21, q22,
    w_sem, sx, sf, sg, rx, sq, rq, skv, rkv, so, ro, s1, rr1, s2, r2sem,
):
    j0 = lax.axis_index("dp")
    e0 = lax.axis_index("ep")
    sib = 1 - e0
    partner = lax.rem(j0 + n_dp // 2, n_dp)
    rows = rg_h.shape[0]
    srows = sg_h.shape[0]
    d_model = rg_h.shape[1]
    ntok = x_s.shape[0]
    half = ntok // 2
    zbs, r2s = (zb0, zb1, zb2), (q20, q21, q22)

    copies = []

    def fetch(src, dst):
        c = pltpu.make_async_copy(src, dst, w_sem.at[len(copies)])
        c.start()
        copies.append(c)
        return c

    c_cache = fetch(cache_h, cache_s)
    c_router = fetch(router_h, router_s)
    gu = []
    for r in range(0, rows, rchunk):
        gu.append((
            r, rchunk, True,
            fetch(rg_h.at[pl.ds(r, rchunk), :], g_s.at[pl.ds(r, rchunk), :]),
            fetch(ru_h.at[pl.ds(r, rchunk), :], u_s.at[pl.ds(r, rchunk), :]),
        ))
    gu.append((
        rows, srows, False,
        fetch(sg_h, g_s.at[pl.ds(rows, srows), :]),
        fetch(su_h, u_s.at[pl.ds(rows, srows), :]),
    ))
    downs = []
    base = 0
    for w in WIDTHS:
        cols = pl.ds(base, CH * w)
        downs.append((
            base, w,
            fetch(rd_h.at[:, cols], d_s.at[pl.ds(0, rows), cols]),
            fetch(sd_h.at[:, cols], d_s.at[pl.ds(rows, srows), cols]),
        ))
        base += CH * w

    tiles = hf.shape[0]
    own = hid_ref[...].astype(F32)
    own_tok = own.shape[0]
    for c in range(CH):
        for i in range(tiles):
            at = (c * tiles + i) * 128
            hf[i, pl.ds(c, own_tok, stride=CH), :] = own[:, at:at + 128]
    for i in range(tiles):
        hsend[:, i * 128:(i + 1) * 128] = hf[i].astype(BF16)

    barrier = pltpu.get_barrier_semaphore()

    def greet(k, _):
        pl.semaphore_signal(barrier, inc=1, device_id={"dp": lax.rem(j0 + k, n_dp)}, device_id_type=MESH)
        return 0

    lax.fori_loop(1, n_dp, greet, 0)
    pl.semaphore_signal(barrier, inc=1, device_id={"ep": sib}, device_id_type=MESH)
    pl.semaphore_wait(barrier, n_dp)

    n_out = n_dp // 2
    out0 = j0 // 2
    in0 = lax.rem(j0, 2)
    across = out0 * 2 + 1 - in0

    def peer(k):
        return lax.rem(out0 + k, n_out) * 2 + in0

    def x_copy(src, j, sem, target):
        return pltpu.make_async_remote_copy(
            src_ref=src, dst_ref=xg.at[e0, j], send_sem=sem, recv_sem=rx.at[e0, j],
            device_id=target, device_id_type=MESH)

    def x_out(k):
        return x_copy(hsend, j0, sx.at[k], {"dp": peer(k)})

    def x_over(k):
        src = hsend if k is None else xg.at[e0, peer(k)]
        j = j0 if k is None else peer(k)
        return x_copy(src, j, sf.at[0 if k is None else k], {"dp": across})

    def x_sib(j, src):
        return x_copy(src, j, sg.at[j], {"ep": sib})

    def arrived(e, j):
        return pltpu.make_async_remote_copy(
            src_ref=hsend, dst_ref=xg.at[e, j], send_sem=sx.at[0], recv_sem=rx.at[e, j],
            device_id={"ep": sib}, device_id_type=MESH)

    def send_out(k, _):
        x_out(k).start()
        return 0

    lax.fori_loop(1, n_out, send_out, 0)
    x_over(None).start()
    x_sib(j0, hsend).start()
    xg[e0, j0] = hsend[...]

    device = j0 * 2 + e0
    own_move = move_ref[device]
    moving = own_move < 2
    slot_b = jnp.where(own_move == 0, 0, 1)
    slot_a = 1 - slot_b
    nq = qsend.shape[0]
    pairs = kk.shape[0] // cache_s.shape[1]
    pages = cache_s.shape[1]
    wide = kk.shape[1]
    win = (wide // 2 + 127) // 128 * 128
    off = wide - win
    shift = wide // 2 - off
    dk = wide // 2

    def attend(q, kv, slot):
        length = len_ref[device * 2 + slot]

        def retile(t, _):
            parts = [
                cache_s[slot, :, pl.ds(pl.multiple_of((2 * t + i) * wide, 128), wide)].astype(F32)
                for i in range(2)
            ]
            kk[pl.ds(pl.multiple_of(2 * pages * t, 16), 2 * pages), :] = (
                jnp.concatenate(parts, axis=0).astype(BF16))
            return 0

        lax.fori_loop(0, pairs // 2, retile, 0)
        qf = q.astype(F32)
        lane = lax.broadcasted_iota(jnp.int32, (nq, win), 1)
        q_even = jnp.where(lane < dk, qf[:nq, :win], 0.0)
        q_odd = jnp.where(lane >= shift, qf[:nq, off:], 0.0)
        qe = jnp.concatenate([q_even, pltpu.roll(q_odd, win - shift, 1)], axis=0)
        qo = jnp.concatenate([pltpu.roll(q_even, shift, 1), q_odd], axis=0)
        s_n = jnp.sum(qe * kv, axis=1, keepdims=True) * SCORE_SCALE
        index = lax.broadcasted_iota(jnp.int32, (1, kk.shape[0]), 1)
        pair = ((index.astype(F32) + 0.5) * (1.0 / pages)).astype(jnp.int32)
        pos = (index - pair * pages) * (2 * pairs) + pair * 2
        s_e = jnp.where(pos < length, contract_last(qe.astype(BF16), kk[:, :win]) * SCORE_SCALE, NEGATIVE)
        s_o = jnp.where(pos + 1 < length, contract_last(qo.astype(BF16), kk[:, off:]) * SCORE_SCALE, NEGATIVE)
        top = jnp.maximum(jnp.max(s_e, axis=1, keepdims=True), jnp.max(s_o, axis=1, keepdims=True))
        top = jnp.maximum(top, s_n)
        p_e, p_o, p_n = jnp.exp(s_e - top), jnp.exp(s_o - top), jnp.exp(s_n - top)
        total = jnp.sum(p_e, axis=1, keepdims=True) + jnp.sum(p_o, axis=1, keepdims=True) + p_n
        o_e = jnp.dot(p_e.astype(BF16), kk[:, :DL], preferred_element_type=F32)
        o_o = jnp.dot(p_o.astype(BF16), kk[:, off:], preferred_element_type=F32)
        out = o_e + pltpu.roll(o_o, win - shift, 1)[:, :DL] + p_n * kv[:, :DL]
        out = out / total
        return jnp.concatenate([out[:nq], out[nq:]], axis=1).astype(BF16)

    qsend[...] = q_ref[slot_b]
    kvs = jnp.concatenate([kv_ref[...].astype(F32), jnp.zeros((kv_ref.shape[0], win - dk), F32)], axis=1)
    kv_b = jnp.where(slot_b == 0, kvs[0:1], kvs[1:2])
    kv_a = jnp.where(slot_b == 0, kvs[1:2], kvs[0:1])
    kvsend[...] = jnp.broadcast_to(kv_b, kvsend.shape).astype(BF16)
    q_copy = pltpu.make_async_remote_copy(
        src_ref=qsend, dst_ref=qrecv, send_sem=sq, recv_sem=rq,
        device_id={"dp": partner}, device_id_type=MESH)
    kv_copy = pltpu.make_async_remote_copy(
        src_ref=kvsend, dst_ref=kvrecv, send_sem=skv, recv_sem=rkv,
        device_id={"dp": partner}, device_id_type=MESH)

    def pass_out(k, _):
        arrived(e0, peer(n_out - k)).wait_recv()
        x_over(n_out - k).start()
        x_sib(peer(n_out - k), xg.at[e0, peer(n_out - k)]).start()
        return 0

    lax.fori_loop(1, n_out, pass_out, 0)
    kv_copy.start()
    q_copy.start()

    def pass_in(k, _):
        j = lax.rem(out0 + n_out - k, n_out) * 2 + 1 - in0
        arrived(e0, j).wait_recv()
        x_sib(j, xg.at[e0, j]).start()
        return 0

    lax.fori_loop(0, n_out, pass_in, 0)

    def settle(k, _):
        arrived(sib, lax.rem(j0 + n_dp - k, n_dp)).wait_recv()
        return 0

    lax.fori_loop(0, n_dp, settle, 0)

    gathered = xg[...].reshape(xf.shape[1], tiles * 128).astype(F32)
    for i in range(tiles):
        xf[i] = gathered[:, i * 128:(i + 1) * 128]
    for c in range(CH):
        for i in range(tiles):
            at = (c * tiles + i) * 128
            x_s[:, at:at + 128] = xf[i, pl.ds(c, ntok, stride=CH), :].astype(BF16)

    c_router.wait()
    n_exp = router_s.shape[0]
    sig = 1.0 / (1.0 + jnp.exp(-contract_last(x_s[...], router_s[...])))
    table = lax.broadcasted_iota(jnp.int32, (ntok, n_exp), 1)
    ids = ids_ref[...]
    table_t = lax.broadcasted_iota(jnp.int32, (n_exp, ntok), 0)
    chosen_t = jnp.zeros((n_exp, ntok), F32)
    for k in range(ids.shape[0]):
        chosen_t += jnp.where(ids[k:k + 1, :] == table_t, 1.0, 0.0)
    row = lax.broadcasted_iota(jnp.int32, (ntok, ntok), 0)
    core = jnp.where(row >= half, 1, 0)
    rest = row - core * half
    token = rest + (rest & ~(own_tok - 1)) + core * own_tok
    perm = jnp.where(token == lax.broadcasted_iota(jnp.int32, (ntok, ntok), 1), 1.0, 0.0)
    chosen = contract_last(perm.astype(BF16), chosen_t.astype(BF16))
    picked = sig * chosen
    expert = (j0 * 2 + e0) * rows // FF
    mine = jnp.sum(jnp.where(table == expert, picked, 0.0), axis=1, keepdims=True)
    row_weight = ROUTE_SCALE * mine / jnp.sum(picked, axis=1, keepdims=True)

    def hidden_units(r, n, routed, cg, cu):
        cg.wait()
        g = contract_last(x_s[...], g_s[pl.ds(r, n), :])
        cu.wait()
        u = contract_last(x_s[...], u_s[pl.ds(r, n), :])
        act = g / (1.0 + jnp.exp(-g)) * u
        if routed:
            act = row_weight * act
        act_s[:, r:r + n] = act.astype(BF16)

    early = min(2, len(gu))
    for args in gu[:early]:
        hidden_units(*args)

    c_cache.wait()
    kv_copy.wait_recv()
    q_copy.wait_recv()
    q_b = jnp.where(moving, qrecv[...].astype(F32), qsend[...].astype(F32))
    kv_b = jnp.where(moving, kvrecv[0:1, :].astype(F32), kv_b)
    osend[...] = attend(q_b, kv_b, slot_b)
    o_copy = pltpu.make_async_remote_copy(
        src_ref=osend, dst_ref=orecv, send_sem=so, recv_sem=ro,
        device_id={"dp": partner}, device_id_type=MESH)
    o_copy.start()

    for args in gu[early:]:
        hidden_units(*args)

    def first_copy(p):
        b, w = downs[p][0], downs[p][1]
        cols = pl.ds(b, CH * w)
        return pltpu.make_async_remote_copy(
            src_ref=ybuf.at[pl.ds(pl.multiple_of(sib * half, 16), half), cols],
            dst_ref=r1.at[:, cols], send_sem=s1.at[p], recv_sem=rr1.at[p],
            device_id={"ep": sib}, device_id_type=MESH)

    def second_copy(p, k):
        j = lax.rem(j0 + k, n_dp)
        return pltpu.make_async_remote_copy(
            src_ref=zbs[p].at[j], dst_ref=r2s[p].at[j0], send_sem=s2.at[p, k], recv_sem=r2sem.at[p, j0],
            device_id={"dp": j}, device_id_type=MESH)

    def second_arrived(p, j):
        return pltpu.make_async_remote_copy(
            src_ref=zbs[p].at[j], dst_ref=r2s[p].at[j], send_sem=s2.at[p, 0], recv_sem=r2sem.at[p, j],
            device_id={"dp": j}, device_id_type=MESH)

    def combine(p):
        b, w = downs[p][0], downs[p][1]
        first_copy(p).wait_recv()
        z = yown[:, b:b + CH * w] + r1[:, b:b + CH * w].astype(F32)
        for c in range(CH):
            for i in range(w // 128):
                at = c * w + i * 128
                zs[i, pl.ds(c, half, stride=CH), :] = z[:, at:at + 128]
        for i in range(w // 128):
            zbs[p][:, :, i * 128:(i + 1) * 128] = zs[i].astype(BF16).reshape(n_dp, -1, 128)

        def send(k, _):
            second_copy(p, k).start()
            return 0

        lax.fori_loop(1, n_dp, send, 0)

    def finish(p):
        b, w = downs[p][0], downs[p][1]

        def add(k, total):
            j = lax.rem(j0 + k, n_dp)
            second_arrived(p, j).wait_recv()
            return total + r2s[p][j].astype(F32)

        total = lax.fori_loop(1, n_dp, add, zbs[p][j0].astype(F32))
        for i in range(w // 128):
            fs[i] = total[:, i * 128:(i + 1) * 128]
        for c in range(CH):
            for i in range(w // 128):
                at = b + c * w + i * 128
                moe_ref[:, at:at + 128] = fs[i, pl.ds(c, own_tok, stride=CH), :].astype(BF16)

    act_all = act_s[...]
    for p, (b, w, c1, c2) in enumerate(downs):
        c1.wait()
        c2.wait()
        y = jnp.dot(act_all, d_s[:, b:b + CH * w], preferred_element_type=F32)
        ybuf[:, b:b + CH * w] = y.astype(BF16)
        yown[:, b:b + CH * w] = jnp.where(e0 == 0, y[:half], y[half:])
        first_copy(p).start()
        if p > 0:
            combine(p - 1)
    combine(len(downs) - 1)
    out_a = attend(q_ref[slot_a], kv_a, slot_a)
    for p in range(len(downs)):
        finish(p)

    o_copy.wait_recv()
    res_a = out_a.astype(F32)
    res_b = jnp.where(moving, orecv[...].astype(F32), osend[...].astype(F32))
    attn_ref[0] = jnp.where(slot_a == 0, res_a, res_b).astype(BF16)
    attn_ref[1] = jnp.where(slot_a == 0, res_b, res_a).astype(BF16)

    q_copy.wait_send()
    kv_copy.wait_send()
    o_copy.wait_send()
    x_over(None).wait_send()

    def drain_out(k, _):
        x_out(k).wait_send()
        x_over(k).wait_send()
        return 0

    lax.fori_loop(1, n_out, drain_out, 0)

    def drain_sib(j, _):
        x_sib(j, hsend).wait_send()
        return 0

    lax.fori_loop(0, n_dp, drain_sib, 0)

    def drain(k, _):
        for p in range(len(downs)):
            second_copy(p, k).wait_send()
        return 0

    lax.fori_loop(1, n_dp, drain, 0)
    for p in range(len(downs)):
        first_copy(p).wait_send()


def local(cache, queries, kv_new, lengths, move_slot, hidden, expert_ids, router,
          routed_gate, routed_up, routed_down, shared_gate, shared_up, shared_down):
    n_dp = lax.axis_size("dp")
    n_ep = lax.axis_size("ep")
    slots, pages, page_len = cache.shape
    dk = kv_new.shape[-1]
    d_model = hidden.shape[-1]
    own_tok = hidden.shape[0] * hidden.shape[1]
    ntok = own_tok * n_dp * n_ep
    half = ntok // 2
    rows, srows = routed_gate.shape[0], shared_gate.shape[0]
    all_rows = rows + srows
    wide = 2 * dk
    nq = queries.shape[-1] // wide
    pairs = page_len // wide
    win = (dk + 127) // 128 * 128
    wmax = max(WIDTHS)
    np_ = len(WIDTHS)
    rchunk = min(rows, 256)
    ncopy = 2 + 2 * (rows // rchunk + 1) + 2 * np_
    vm = pl.BlockSpec(memory_space=pltpu.VMEM)
    hb = pl.BlockSpec(memory_space=pl.ANY)
    dma = pltpu.SemaphoreType.DMA
    attn, moe = pl.pallas_call(
        functools.partial(kernel, n_dp, rchunk),
        out_shape=(
            jax.ShapeDtypeStruct((slots, nq, 2 * DL), BF16),
            jax.ShapeDtypeStruct((own_tok, d_model), BF16),
        ),
        in_specs=[pl.BlockSpec(memory_space=pltpu.SMEM)] * 2 + [vm] * 4 + [hb] * 8,
        out_specs=(vm, vm),
        scratch_shapes=[
            pltpu.VMEM(cache.shape, BF16),
            pltpu.VMEM(router.shape, BF16),
            pltpu.VMEM((all_rows, d_model), BF16),
            pltpu.VMEM((all_rows, d_model), BF16),
            pltpu.VMEM((all_rows, d_model), BF16),
            pltpu.VMEM((d_model // CH // 128, own_tok * CH, 128), F32),
            pltpu.VMEM((own_tok * CH, d_model // CH), BF16),
            pltpu.VMEM((n_ep, n_dp, own_tok * CH, d_model // CH), BF16),
            pltpu.VMEM((d_model // CH // 128, ntok * CH, 128), F32),
            pltpu.VMEM((ntok, d_model), BF16),
            pltpu.VMEM((ntok, all_rows), BF16),
            pltpu.VMEM((pairs * pages, wide), BF16),
            pltpu.VMEM((nq, wide), BF16),
            pltpu.VMEM((nq, wide), BF16),
            pltpu.VMEM((16, win), BF16),
            pltpu.VMEM((16, win), BF16),
            pltpu.VMEM((nq, 2 * DL), BF16),
            pltpu.VMEM((nq, 2 * DL), BF16),
            pltpu.VMEM((ntok, d_model), BF16),
            pltpu.VMEM((half, d_model), F32),
            pltpu.VMEM((half, d_model), BF16),
            pltpu.VMEM((wmax // 128, half * CH, 128), F32),
            pltpu.VMEM((wmax // 128, own_tok * CH, 128), F32),
        ]
        + [pltpu.VMEM((n_dp, own_tok * CH, w), BF16) for w in WIDTHS] * 2
        + [
            dma((ncopy,)), dma((n_dp,)), dma((n_dp,)), dma((n_dp,)), dma((n_ep, n_dp)),
            dma, dma, dma, dma, dma, dma,
            dma((np_,)), dma((np_,)), dma((np_, n_dp)), dma((np_, n_dp)),
        ],
        compiler_params=pltpu.CompilerParams(
            collective_id=0, has_side_effects=True, vmem_limit_bytes=63 * 1024 * 1024),
    )(lengths, move_slot, queries.reshape(slots, nq, wide), kv_new.reshape(slots, dk),
      hidden.reshape(own_tok, d_model), expert_ids.reshape(ntok, -1).T, cache, router, routed_gate, routed_up, routed_down,
      shared_gate, shared_up, shared_down)
    return (attn.reshape(slots, 1, nq * 2 * DL), moe.reshape(hidden.shape))


def solution(mesh):
    row = P(("grp", "dp", "ep"), None, None)
    weight = P(("dp", "ep"), None)
    in_specs = (row, row, row, P("grp"), P("grp"), row, P("grp", None, None), P()) + (weight,) * 6
    return jax.shard_map(local, mesh=mesh, in_specs=in_specs, out_specs=(row, row), check_vma=False)
```
